32 devices in a mesh: seg: 4 (over y, x), pen: 8 (over z, core).
Axes of the slice: x: 2, y: 2, z: 4, core: 2. Of those that a mesh axis runs over, the one named last changes fastest.
Arguments:
- state: float32 [16, 384, 384], P('seg', 'pen'), may hold values from -6 to 6
- krylov: float32 [16, 16, 384, 384], P(None, 'seg', 'pen'), may hold values from -15 to 15
Outputs:
- residual: float32 [16, 384, 384], P('seg', 'pen')
- next_vector: float32 [16, 384, 384], P('seg', 'pen')
- hessenberg: float32 [17], replicated
The draws below stay inside these ranges and needn't reach their ends.
All inputs are finite; a program needn't handle non-finite values.
Results may differ from the reference program's by a relative error of at most 0.0003.
Values sent between devices are 32-bit elements; how exact they have to be, the bound alone decides.
A program may use at most 64 MiB of HBM per device.

```python
import math
import jax
import jax.numpy as jnp
from jax import lax

NX = 384
NZ = 384
PLANES = 4
STEPS = 2
KRY = 16
SEGMENTS = 4
ROWS = 16


def draw_state(key, part):
    first_key = jax.random.fold_in(key, 0)
    return jax.random.truncated_normal(first_key, -6.0, 6.0, (ROWS, NZ, NX), jnp.float32)


def draw_krylov(key, part):
    first_key, second_key = jax.random.split(jax.random.fold_in(key, 17))
    values = jax.random.truncated_normal(first_key, -4.0, 4.0, (KRY, ROWS, NZ, NX), jnp.float32)
    mixing = jax.random.uniform(second_key, (KRY,), jnp.float32, 0.05, 0.25)
    mixing = jnp.where(jnp.arange(KRY) == KRY - 1, 0.0, mixing)
    segment = (jnp.arange(ROWS) // PLANES).astype(jnp.float32)
    rise_seg = jnp.sqrt(1.0 + 2.0 * segment / max(SEGMENTS - 1, 1))
    rise_z = jnp.sqrt(1.0 + 2.0 * jnp.arange(NZ).astype(jnp.float32) / (NZ - 1))
    mixed = values + mixing[:, None, None, None] * values[KRY - 1][None]
    return mixed * rise_seg[None, :, None, None] * rise_z[None, None, :, None]


def setup_inputs(seed: int = 0) -> dict:
    key_of = jax.random.split(jax.random.key(seed), 3)
    return {
        "state": draw_state(jax.random.fold_in(key_of[2], 71), 0),
        "krylov": draw_krylov(jax.random.fold_in(key_of[2], 71), 0),
    }


time_step = 0.0003
viscosity = 0.0226

def product(formula, former, latter):
    return jnp.einsum(formula, former, latter, precision=lax.Precision.HIGHEST, preferred_element_type=jnp.float32)

def tables(count):
    indices = jnp.arange(count, dtype=jnp.int32)
    phases = indices[:, None] * indices[None, :] % count
    angles = phases.astype(jnp.float32) * (2.0 * math.pi / count)
    cosines = jnp.cos(angles)
    sines = jnp.sin(angles)
    signed = jnp.where(indices <= count // 2, indices, indices - count).astype(jnp.float32)
    slopes = jnp.where(indices == count // 2, 0.0, signed)
    return (cosines + sines, slopes[:, None] * (cosines - sines), signed)

def tendency(z_slope, z_plain):
    stream_z = z_slope[0:2]
    vortex_z = z_slope[2:4]
    stream_x = z_plain[0:2]
    vortex_x = z_plain[2:4]
    base_term = stream_x[0] * vortex_z[0] - stream_z[0] * vortex_x[0]
    tangent_term = stream_x[1] * vortex_z[0] + stream_x[0] * vortex_z[1] - stream_z[1] * vortex_x[0] - stream_z[0] * vortex_x[1]
    return jnp.stack([base_term, tangent_term])

def reference(state, krylov):
    basis_x, slopes_x, signed_x = tables(NX)
    basis_z, slopes_z, signed_z = tables(NZ)
    ksquare = signed_z[:, None] ** 2 + signed_x[None, :] ** 2
    inverse_k = jnp.where(ksquare > 0, 1.0 / jnp.where(ksquare > 0, ksquare, 1.0), 0.0)
    damping = 1.0 / (1.0 + time_step * viscosity * ksquare)
    forward_x = basis_x / NX
    forward_z = basis_z / NZ
    direction = krylov[KRY - 1]
    fields = jnp.stack([state, direction])
    for repeat in range(STEPS):
        spectra = jnp.concatenate([fields * inverse_k, fields], 0)
        values_x = product('arzx,xj->arzj', spectra, basis_x)
        slopes_along = product('arzx,xj->arzj', spectra, slopes_x)
        z_slope = product('arzx,zj->arjx', values_x, slopes_z)
        z_plain = product('arzx,zj->arjx', slopes_along, basis_z)
        modes_z = product('arzx,zk->arkx', tendency(z_slope, z_plain), forward_z)
        forcing = product('arzx,xk->arzk', modes_z, forward_x)
        fields = (fields + time_step * forcing) * damping
    moved = jnp.roll(fields, PLANES, axis=1)
    residual = moved[0] - state
    image = moved[1] - direction
    total = float(ROWS * NZ * NX)
    coeffs = product('krzx,rzx->k', krylov, image) / total
    remain = image - product('k,krzx->rzx', coeffs, krylov)
    norm_value = jnp.sqrt(jnp.sum(remain * remain) / total + 1e-06)
    return (residual, remain / norm_value, jnp.concatenate([coeffs, norm_value[None]]))
```

```python
import functools
import math

import jax
import jax.numpy as jnp
import ml_dtypes
import numpy as np
from jax import lax
from jax.experimental import pallas as pl
from jax.experimental.pallas import tpu as pltpu
from jax.sharding import PartitionSpec as P

STEPS = 2
MESH = pl.DeviceIdType.MESH


time_step = 0.0003
viscosity = 0.0226


def shifted(block, axis, distance):
    devices = range(lax.axis_size(axis))
    route = [((i - distance) % len(devices), i) for i in devices]
    return lax.ppermute(block, axis, route)


def product(formula, former, latter):
    return jnp.einsum(
        formula, former, latter, precision=lax.Precision.HIGHEST, preferred_element_type=jnp.float32
    )


def tables(count):
    indices = jnp.arange(count, dtype=jnp.int32)
    phases = indices[:, None] * indices[None, :] % count
    angles = phases.astype(jnp.float32) * (2.0 * math.pi / count)
    cosines = jnp.cos(angles)
    sines = jnp.sin(angles)
    signed = jnp.where(indices <= count // 2, indices, indices - count).astype(jnp.float32)
    slopes = jnp.where(indices == count // 2, 0.0, signed)
    return (cosines + sines, slopes[:, None] * (cosines - sines), signed)


def tendency(z_slope, z_plain):
    stream_z = z_slope[0:2]
    vortex_z = z_slope[2:4]
    stream_x = z_plain[0:2]
    vortex_x = z_plain[2:4]
    base_term = stream_x[0] * vortex_z[0] - stream_z[0] * vortex_x[0]
    tangent_term = (
        stream_x[1] * vortex_z[0]
        + stream_x[0] * vortex_z[1]
        - stream_z[1] * vortex_x[0]
        - stream_z[0] * vortex_x[1]
    )
    return jnp.stack([base_term, tangent_term])


def advance(fields, inverse_k, damping, basis_x, slopes_x, basis_z, slopes_z, forward_x, forward_z):
    spectra = jnp.concatenate([fields * inverse_k, fields], 0)
    values_x = product("arzx,xj->arzj", spectra, basis_x)
    slopes_along = product("arzx,xj->arzj", spectra, slopes_x)
    z_slope = product(
        "arzx,zj->arxj",
        lax.all_to_all(values_x, "pen", split_axis=3, concat_axis=2, tiled=True),
        slopes_z,
    )
    z_plain = product(
        "arzx,zj->arxj",
        lax.all_to_all(slopes_along, "pen", split_axis=3, concat_axis=2, tiled=True),
        basis_z,
    )
    modes_z = product("arxz,zk->arxk", tendency(z_slope, z_plain), forward_z)
    returned = lax.all_to_all(modes_z, "pen", split_axis=3, concat_axis=2, tiled=True)
    forcing = product("arxz,xk->arzk", returned, forward_x)
    return (fields + time_step * forcing) * damping


def body(state, krylov):
    rank = lax.axis_index("pen")
    zcut = state.shape[1]
    planes = state.shape[0]
    modes_x = state.shape[2]
    modes_z = state.shape[1] * lax.axis_size("pen")
    basis_x, slopes_x, signed_x = tables(state.shape[2])
    basis_z, slopes_z, signed_z = tables(zcut * lax.axis_size("pen"))
    local_z = lax.dynamic_slice_in_dim(signed_z, rank * zcut, zcut)
    ksquare = local_z[:, None] ** 2 + signed_x[None, :] ** 2
    inverse_k = jnp.where(ksquare > 0, 1.0 / jnp.where(ksquare > 0, ksquare, 1.0), 0.0)
    damping = 1.0 / (1.0 + time_step * viscosity * ksquare)
    forward_x = basis_x / modes_x
    forward_z = basis_z / modes_z
    direction = krylov[-1]
    fields = jnp.stack([state, direction])
    for repeat in range(STEPS):
        fields = advance(
            fields, inverse_k, damping, basis_x, slopes_x, basis_z, slopes_z, forward_x, forward_z
        )
    moved = shifted(fields, "seg", 1)
    residual = moved[0] - state
    image = moved[1] - direction
    total = float(lax.axis_size("seg") * planes * modes_z * modes_x)
    local_dots = product("krzx,rzx->k", krylov, image)
    gram_local = product("krzx,jrzx->kj", krylov, krylov)
    summed, energy, gram = lax.psum(
        (local_dots, jnp.sum(image * image), gram_local), ("seg", "pen")
    )
    coeffs = summed / total
    quadratic = jnp.dot(
        coeffs,
        jnp.dot(gram, coeffs, precision=lax.Precision.HIGHEST),
        precision=lax.Precision.HIGHEST,
    )
    squared = energy - 2.0 * jnp.dot(coeffs, summed, precision=lax.Precision.HIGHEST) + quadratic
    remain = image - product("k,krzx->rzx", coeffs, krylov)
    norm_value = jnp.sqrt(squared / total + 1e-06)
    return (residual, remain / norm_value, jnp.concatenate([coeffs, norm_value[None]]))


def split(values):
    high = values.astype(jnp.bfloat16)
    low = (values - high.astype(jnp.float32)).astype(jnp.bfloat16)
    return high, low


def host_split(values):
    values = values.astype(np.float32)
    high = values.astype(ml_dtypes.bfloat16)
    low = (values - high.astype(np.float32)).astype(ml_dtypes.bfloat16)
    return high, low


def left_table(values):
    high, low = host_split(values)
    return np.concatenate([high, low, high], -1)


def right_table(values):
    high, low = host_split(values)
    return np.concatenate([high, high, low], -2)


def host_tables(count):
    indices = np.arange(count)
    angles = 2.0 * np.pi * (indices[:, None] * indices[None, :] % count) / count
    signed = np.where(indices <= count // 2, indices, indices - count).astype(np.float64)
    slopes = np.where(indices == count // 2, 0.0, signed)
    cas = np.cos(angles) + np.sin(angles)
    return cas, np.cos(angles) - np.sin(angles), slopes, signed


def constants(modes_z, modes_x):
    cas_z, turned_z, _, signed_z = host_tables(modes_z)
    cas_x, turned_x, slopes_x, signed_x = host_tables(modes_x)
    slope_x = slopes_x[:, None] * turned_x
    half = modes_z // 2
    into = [
        left_table(np.concatenate([cas_z[:half, c::2].T, turned_z[:half, c::2].T], 0))
        for c in range(2)
    ]
    back = [left_table(cas_z[:half, c::2]) for c in range(2)]
    ksq = signed_z[:, None] ** 2 + signed_x[None, :] ** 2
    inverse = np.where(ksq > 0, 1.0 / np.where(ksq > 0, ksq, 1.0), 0.0).astype(np.float32)
    damping = (1.0 / (1.0 + time_step * viscosity * ksq)).astype(np.float32)
    return (
        np.stack(into), np.stack(back), right_table(cas_x), right_table(slope_x), inverse, damping
    )


def kernel(
    segs, pens,
    state_hbm, krylov_hbm, into_hbm, back_hbm, cas_hbm, slope_hbm, inverse_hbm, damping_hbm,
    residual_ref, next_ref, hess_ref,
    stored, start, into_t, back_t, cas_t, slope_t, inverse, damping,
    field, wide, tall, base, tangent, mine, theirs, ending, arrived, image,
    accum, pay, gather_pen, gather_seg, spread, pay_n, norm_pen, norm_seg,
    load_sem, local_sem, in_send, in_recv, fwd_send, swap_send, swap_recv,
    out_send, out_recv, pen_send, pen_recv, seg_send, seg_recv,
):
    seg = lax.axis_index("seg")
    pen = lax.axis_index("pen")
    planes, cut, modes_x = stored.shape[1:]
    kry = stored.shape[0]
    modes_z = cut * pens
    half = modes_z // 2
    chip = pen // 2
    core = pen % 2
    sibling = chip * 2 + 1 - core
    following = lax.rem(seg + 1, segs)
    preceding = lax.rem(seg + segs - 1, segs)

    def remote(src, dst, send, recv, to_seg, to_pen):
        return pltpu.make_async_remote_copy(
            src_ref=src, dst_ref=dst, send_sem=send, recv_sem=recv,
            device_id=(to_seg, to_pen), device_id_type=MESH,
        )

    def rows(owner):
        return pl.ds(pl.multiple_of(owner * cut, cut), cut)

    loads = [
        pltpu.make_async_copy(src, dst, load_sem.at[i])
        for i, (src, dst) in enumerate([
            (inverse_hbm, inverse), (into_hbm.at[core], into_t), (cas_hbm, cas_t),
            (slope_hbm, slope_t), (back_hbm.at[core], back_t), (damping_hbm, damping),
            (state_hbm, start), (krylov_hbm, stored),
        ])
    ]
    for load in loads:
        load.start()

    barrier = pltpu.get_barrier_semaphore()

    def greet(to_seg, to_pen):
        pl.semaphore_signal(barrier, inc=1, device_id=(to_seg, to_pen), device_id_type=MESH)

    for i in range(1, pens):
        greet(seg, lax.rem(pen + i, pens))
    for i in range(planes):
        greet(following, core * planes + i)
        greet(preceding, i * 2 + pen // planes)
    for i in range(1, segs):
        greet(lax.rem(seg + i, segs), pen)
    pl.semaphore_wait(barrier, pens - 1 + 2 * planes + segs - 1)

    sources = [lambda plane: state_hbm.at[plane], lambda plane: krylov_hbm.at[kry - 1, plane]]
    pending = []
    own = []
    for f in range(2):
        for i in range(1, planes):
            plane = lax.rem(chip + i, planes)
            copy = remote(
                sources[f](plane), field.at[f, rows(pen)], in_send.at[f, i], in_recv.at[f, pen],
                seg, plane * 2 + core,
            )
            copy.start()
            pending.append(copy)
        copy = remote(
            sources[f](chip), field.at[f, rows(pen)], in_send.at[f, 0], in_recv.at[f, pen],
            seg, sibling,
        )
        copy.start()
        pending.append(copy)
        copy = pltpu.make_async_copy(sources[f](chip), field.at[f, rows(pen)], local_sem.at[f])
        copy.start()
        own.append(copy)

    def awaited(f, owner):
        place = field.at[f, rows(owner)]
        remote(place, place, in_send.at[f, 0], in_recv.at[f, owner], seg, sibling).wait_recv()

    forwards = [[], []]

    def relay(f):
        for i in range(1, planes):
            owner = lax.rem(chip + i, planes) * 2 + core
            awaited(f, owner)
            place = field.at[f, rows(owner)]
            copy = remote(
                place, place, fwd_send.at[f, i], in_recv.at[f, owner], seg, sibling
            )
            copy.start()
            forwards[f].append(copy)

    def complete(f):
        own[f].wait()
        for i in range(planes):
            awaited(f, lax.rem(chip + i, planes) * 2 + 1 - core)

    sign = (1 - 2 * core).astype(jnp.float32)

    number = lax.broadcasted_iota(jnp.int32, (half, 1), 0)
    slope_top = number.astype(jnp.float32)
    slope_low = jnp.where(number == 0, 0, number - half).astype(jnp.float32)

    def derive(f, out):
        for way, table in ((0, slope_t), (1, cas_t)):
            for part in range(2):
                top = field[f, 0:half, :]
                low = field[f, half:modes_z, :]
                if part == 0:
                    top = top * inverse[0:half, :]
                    low = low * inverse[half:modes_z, :]
                if way == 1:
                    top = top * slope_top
                    low = low * slope_low
                high, rest = split(top + sign * low)
                lanes = slice(part * modes_x, (part + 1) * modes_x)
                wide[0:half, lanes] = high
                wide[half:modes_z, lanes] = high
                wide[modes_z:modes_z + half, lanes] = rest
            mixed = jnp.dot(
                into_t[way * half:(way + 1) * half, :], wide[...],
                preferred_element_type=jnp.float32,
            )
            for part in range(2):
                lines = slice(part * half, (part + 1) * half)
                high, rest = split(mixed[:, part * modes_x:(part + 1) * modes_x])
                tall[lines, 0:modes_x] = high
                tall[lines, modes_x:2 * modes_x] = rest
                tall[lines, 2 * modes_x:3 * modes_x] = high
            out[way] = jnp.dot(tall[...], table[...], preferred_element_type=jnp.float32)

    def swap(f, step):
        n = step * 2 + f
        return remote(
            mine.at[n], theirs.at[n], swap_send.at[n], swap_recv.at[n], seg, sibling
        )

    def give_back(f, step, value):
        high, rest = split(value)
        lanes = slice(0, modes_x)
        wide[0:half, lanes] = high
        wide[half:modes_z, lanes] = high
        wide[modes_z:modes_z + half, lanes] = rest
        mixed = jnp.dot(back_t[...], wide[:, lanes], preferred_element_type=jnp.float32)
        high, rest = split(mixed)
        lines = slice(0, half)
        tall[lines, 0:modes_x] = high
        tall[lines, modes_x:2 * modes_x] = rest
        tall[lines, 2 * modes_x:3 * modes_x] = high
        mine[step * 2 + f] = jnp.dot(
            tall[lines, :], cas_t[...], preferred_element_type=jnp.float32
        )
        swap(f, step).start()

    def base_step(step):
        derive(0, base)
        upper, lower = slice(0, half), slice(half, modes_z)
        give_back(0, step, base[0, upper] * base[1, lower] - base[1, upper] * base[0, lower])

    def tangent_step(step):
        derive(1, tangent)
        upper, lower = slice(0, half), slice(half, modes_z)
        give_back(
            1, step,
            tangent[0, upper] * base[1, lower] + base[0, upper] * tangent[1, lower]
            - tangent[1, upper] * base[0, lower] - base[1, upper] * tangent[0, lower],
        )

    scale = time_step / (modes_z * modes_x)

    def update(f, step):
        n = step * 2 + f
        swap(f, step).wait()
        own_part = mine[n] * scale
        other = theirs[n] * scale
        field[f, 0:half, :] = (field[f, 0:half, :] + (own_part + other)) * damping[0:half, :]
        field[f, half:modes_z, :] = (
            field[f, half:modes_z, :] + sign * (own_part - other)
        ) * damping[half:modes_z, :]

    def finish(f):
        n = (STEPS - 1) * 2 + f
        swap(f, STEPS - 1).wait()
        part = pl.ds(pl.multiple_of(core * half, half), half)
        change = jnp.where(core == 0, mine[n] + theirs[n], theirs[n] - mine[n])
        ending[f] = (field[f, part, :] + scale * change) * damping[part, :]
        for i in range(planes):
            copy = remote(
                ending.at[f, i * cut:(i + 1) * cut], arrived.at[f, chip],
                out_send.at[f, i], out_recv.at[f, chip], following, core * planes + i,
            )
            copy.start()
            pending.append(copy)

    relay(0)
    for load in loads[:5]:
        load.wait()
    complete(0)
    base_step(0)
    relay(1)
    complete(1)
    tangent_step(0)
    loads[5].wait()
    for f in range(2):
        for copy in forwards[f]:
            copy.wait_send()
    for step in range(1, STEPS):
        update(0, step - 1)
        base_step(step)
        update(1, step - 1)
        if step == STEPS - 1:
            finish(0)
        tangent_step(step)
    finish(1)
    loads[6].wait()
    loads[7].wait()

    def landed(f, plane):
        remote(
            ending.at[f, 0:cut], arrived.at[f, plane], out_send.at[f, 0], out_recv.at[f, plane],
            following, pen,
        ).wait_recv()

    for plane in range(planes):
        landed(0, plane)
        residual_ref[plane] = arrived[0, plane] - start[plane]

    def fold(values):
        summed = jnp.sum(values.reshape(cut // 8, 8, modes_x), axis=0)
        total = summed[:, 0:128]
        for lane in range(128, modes_x, 128):
            total = total + summed[:, lane:lane + 128]
        return total

    for plane in range(planes):
        landed(1, plane)
        image[plane] = arrived[1, plane] - stored[kry - 1, plane]

    accum[...] = jnp.zeros_like(accum)

    def dots(plane, _):
        values = image[plane]
        for k in range(kry):
            accum[k] += fold(stored[k, plane] * values)
        return 0

    lax.fori_loop(0, planes, dots, 0)
    pay[0] = jnp.sum(accum[...], axis=1)

    def gather(source, over_pen, over_seg, turn):
        over_pen[pen] = source[0]
        copies = []
        for i in range(1, pens):
            copy = remote(
                source.at[0], over_pen.at[pen], pen_send.at[turn, i], pen_recv.at[turn, pen],
                seg, lax.rem(pen + i, pens),
            )
            copy.start()
            copies.append(copy)
        for i in range(1, pens):
            owner = lax.rem(pen + i, pens)
            remote(
                source.at[0], over_pen.at[owner], pen_send.at[turn, i],
                pen_recv.at[turn, owner], seg, owner,
            ).wait_recv()
        source[1] = jnp.sum(over_pen[...], axis=0)
        over_seg[seg] = source[1]
        for i in range(1, segs):
            copy = remote(
                source.at[1], over_seg.at[seg], seg_send.at[turn, i], seg_recv.at[turn, seg],
                lax.rem(seg + i, segs), pen,
            )
            copy.start()
            copies.append(copy)
        for i in range(1, segs):
            owner = lax.rem(seg + i, segs)
            remote(
                source.at[1], over_seg.at[owner], seg_send.at[turn, i],
                seg_recv.at[turn, owner], owner, pen,
            ).wait_recv()
        pending.extend(copies)
        return jnp.sum(over_seg[...], axis=0)

    total = float(segs * planes * modes_z * modes_x)
    coeffs = jnp.sum(gather(pay, gather_pen, gather_seg, 0), axis=1, keepdims=True) / total
    spread[...] = jnp.broadcast_to(coeffs, spread.shape)
    hess_ref[0:kry] = spread[...]

    pay_n[0] = jnp.zeros_like(pay_n[0])

    def remains(plane, _):
        values = image[plane]
        for k in range(kry):
            values = values - spread[k:k + 1, 0:1] * stored[k, plane]
        image[plane] = values
        pay_n[0] += fold(values * values)
        return 0

    lax.fori_loop(0, planes, remains, 0)
    squared = jnp.sum(gather(pay_n, norm_pen, norm_seg, 1), keepdims=True)
    norm = jnp.sqrt(squared / total + 1e-06)
    hess_ref[kry:kry + 8] = jnp.broadcast_to(norm, (8, 128))
    factor = 1.0 / norm
    for plane in range(planes):
        next_ref[plane] = image[plane] * factor
    for copy in pending:
        copy.wait_send()


def fused(state, krylov, *, tables_of, segs, pens):
    planes, cut, modes_x = state.shape
    kry = krylov.shape[0]
    modes_z = cut * pens
    half = modes_z // 2
    f32, bf16 = jnp.float32, jnp.bfloat16
    dma = pltpu.SemaphoreType.DMA
    vmem = pltpu.VMEM
    residual, next_vector, hess = pl.pallas_call(
        functools.partial(kernel, segs, pens),
        out_shape=(
            jax.ShapeDtypeStruct(state.shape, f32),
            jax.ShapeDtypeStruct(state.shape, f32),
            jax.ShapeDtypeStruct((kry + 8, 128), f32),
        ),
        in_specs=[pl.BlockSpec(memory_space=pl.ANY)] * 8,
        out_specs=(pl.BlockSpec(memory_space=pltpu.VMEM),) * 3,
        scratch_shapes=[
            vmem(krylov.shape, f32),
            vmem(state.shape, f32),
            vmem((modes_z, 3 * half), bf16),
            vmem((half, 3 * half), bf16),
            vmem((3 * modes_x, modes_x), bf16),
            vmem((3 * modes_x, modes_x), bf16),
            vmem((modes_z, modes_x), f32),
            vmem((modes_z, modes_x), f32),
            vmem((2, modes_z, modes_x), f32),
            vmem((3 * half, 2 * modes_x), bf16),
            vmem((modes_z, 3 * modes_x), bf16),
            vmem((2, modes_z, modes_x), f32),
            vmem((2, modes_z, modes_x), f32),
            vmem((2 * STEPS, half, modes_x), f32),
            vmem((2 * STEPS, half, modes_x), f32),
            vmem((2, half, modes_x), f32),
            vmem((2, planes, cut, modes_x), f32),
            vmem((planes, cut, modes_x), f32),
            vmem((kry, 8, 128), f32),
            vmem((2, kry, 128), f32),
            vmem((pens, kry, 128), f32),
            vmem((segs, kry, 128), f32),
            vmem((kry, 128), f32),
            vmem((2, 8, 128), f32),
            vmem((pens, 8, 128), f32),
            vmem((segs, 8, 128), f32),
            dma((8,)),
            dma((2,)),
            dma((2, planes)),
            dma((2, pens)),
            dma((2, planes)),
            dma((2 * STEPS,)),
            dma((2 * STEPS,)),
            dma((2, planes)),
            dma((2, planes)),
            dma((2, pens)),
            dma((2, pens)),
            dma((2, segs)),
            dma((2, segs)),
        ],
        compiler_params=pltpu.CompilerParams(
            collective_id=0, has_side_effects=True, vmem_limit_bytes=50 * 1024 * 1024
        ),
    )(state, krylov, *[jnp.asarray(t) for t in tables_of])
    return residual, next_vector, hess[:kry + 1, 0]


def solution(mesh):
    segs, pens = mesh.shape["seg"], mesh.shape["pen"]

    def whole(state, krylov):
        rows, modes_z, modes_x = state.shape
        planes, cut = rows // segs, modes_z // pens
        local = body
        if (
            pens == 2 * planes
            and cut % 8 == 0
            and modes_z % 32 == 0
            and modes_x % 128 == 0
            and krylov.shape[0] % 8 == 0
        ):
            local = functools.partial(
                fused, tables_of=constants(modes_z, modes_x), segs=segs, pens=pens
            )
        return jax.shard_map(
            local,
            mesh=mesh,
            in_specs=(P("seg", "pen", None), P(None, "seg", "pen", None)),
            out_specs=(P("seg", "pen", None), P("seg", "pen", None), P()),
            check_vma=False,
        )(state, krylov)

    return whole
```

```python
import functools
import math

import jax
import jax.numpy as jnp
import ml_dtypes
import numpy as np
from jax import lax
from jax.experimental import pallas as pl
from jax.experimental.pallas import tpu as pltpu
from jax.sharding import PartitionSpec as P

STEPS = 2
MESH = pl.DeviceIdType.MESH


time_step = 0.0003
viscosity = 0.0226


def shifted(block, axis, distance):
    devices = range(lax.axis_size(axis))
    route = [((i - distance) % len(devices), i) for i in devices]
    return lax.ppermute(block, axis, route)


def product(formula, former, latter):
    return jnp.einsum(
        formula, former, latter, precision=lax.Precision.HIGHEST, preferred_element_type=jnp.float32
    )


def tables(count):
    indices = jnp.arange(count, dtype=jnp.int32)
    phases = indices[:, None] * indices[None, :] % count
    angles = phases.astype(jnp.float32) * (2.0 * math.pi / count)
    cosines = jnp.cos(angles)
    sines = jnp.sin(angles)
    signed = jnp.where(indices <= count // 2, indices, indices - count).astype(jnp.float32)
    slopes = jnp.where(indices == count // 2, 0.0, signed)
    return (cosines + sines, slopes[:, None] * (cosines - sines), signed)


def tendency(z_slope, z_plain):
    stream_z = z_slope[0:2]
    vortex_z = z_slope[2:4]
    stream_x = z_plain[0:2]
    vortex_x = z_plain[2:4]
    base_term = stream_x[0] * vortex_z[0] - stream_z[0] * vortex_x[0]
    tangent_term = (
        stream_x[1] * vortex_z[0]
        + stream_x[0] * vortex_z[1]
        - stream_z[1] * vortex_x[0]
        - stream_z[0] * vortex_x[1]
    )
    return jnp.stack([base_term, tangent_term])


def advance(fields, inverse_k, damping, basis_x, slopes_x, basis_z, slopes_z, forward_x, forward_z):
    spectra = jnp.concatenate([fields * inverse_k, fields], 0)
    values_x = product("arzx,xj->arzj", spectra, basis_x)
    slopes_along = product("arzx,xj->arzj", spectra, slopes_x)
    z_slope = product(
        "arzx,zj->arxj",
        lax.all_to_all(values_x, "pen", split_axis=3, concat_axis=2, tiled=True),
        slopes_z,
    )
    z_plain = product(
        "arzx,zj->arxj",
        lax.all_to_all(slopes_along, "pen", split_axis=3, concat_axis=2, tiled=True),
        basis_z,
    )
    modes_z = product("arxz,zk->arxk", tendency(z_slope, z_plain), forward_z)
    returned = lax.all_to_all(modes_z, "pen", split_axis=3, concat_axis=2, tiled=True)
    forcing = product("arxz,xk->arzk", returned, forward_x)
    return (fields + time_step * forcing) * damping


def body(state, krylov):
    rank = lax.axis_index("pen")
    zcut = state.shape[1]
    planes = state.shape[0]
    modes_x = state.shape[2]
    modes_z = state.shape[1] * lax.axis_size("pen")
    basis_x, slopes_x, signed_x = tables(state.shape[2])
    basis_z, slopes_z, signed_z = tables(zcut * lax.axis_size("pen"))
    local_z = lax.dynamic_slice_in_dim(signed_z, rank * zcut, zcut)
    ksquare = local_z[:, None] ** 2 + signed_x[None, :] ** 2
    inverse_k = jnp.where(ksquare > 0, 1.0 / jnp.where(ksquare > 0, ksquare, 1.0), 0.0)
    damping = 1.0 / (1.0 + time_step * viscosity * ksquare)
    forward_x = basis_x / modes_x
    forward_z = basis_z / modes_z
    direction = krylov[-1]
    fields = jnp.stack([state, direction])
    for repeat in range(STEPS):
        fields = advance(
            fields, inverse_k, damping, basis_x, slopes_x, basis_z, slopes_z, forward_x, forward_z
        )
    moved = shifted(fields, "seg", 1)
    residual = moved[0] - state
    image = moved[1] - direction
    total = float(lax.axis_size("seg") * planes * modes_z * modes_x)
    local_dots = product("krzx,rzx->k", krylov, image)
    gram_local = product("krzx,jrzx->kj", krylov, krylov)
    summed, energy, gram = lax.psum(
        (local_dots, jnp.sum(image * image), gram_local), ("seg", "pen")
    )
    coeffs = summed / total
    quadratic = jnp.dot(
        coeffs,
        jnp.dot(gram, coeffs, precision=lax.Precision.HIGHEST),
        precision=lax.Precision.HIGHEST,
    )
    squared = energy - 2.0 * jnp.dot(coeffs, summed, precision=lax.Precision.HIGHEST) + quadratic
    remain = image - product("k,krzx->rzx", coeffs, krylov)
    norm_value = jnp.sqrt(squared / total + 1e-06)
    return (residual, remain / norm_value, jnp.concatenate([coeffs, norm_value[None]]))


def split(values):
    high = values.astype(jnp.bfloat16)
    low = (values - high.astype(jnp.float32)).astype(jnp.bfloat16)
    return high, low


def host_split(values):
    values = values.astype(np.float32)
    high = values.astype(ml_dtypes.bfloat16)
    low = (values - high.astype(np.float32)).astype(ml_dtypes.bfloat16)
    return high, low


def left_table(values):
    high, low = host_split(values)
    return np.concatenate([high, low, high], -1)


def right_table(values):
    high, low = host_split(values)
    return np.concatenate([high, high, low], -2)


def host_tables(count):
    indices = np.arange(count)
    angles = 2.0 * np.pi * (indices[:, None] * indices[None, :] % count) / count
    signed = np.where(indices <= count // 2, indices, indices - count).astype(np.float64)
    slopes = np.where(indices == count // 2, 0.0, signed)
    cas = np.cos(angles) + np.sin(angles)
    return cas, np.cos(angles) - np.sin(angles), slopes, signed


def constants(modes_z, modes_x):
    cas_z, turned_z, _, signed_z = host_tables(modes_z)
    cas_x, turned_x, slopes_x, signed_x = host_tables(modes_x)
    slope_x = slopes_x[:, None] * turned_x
    half = modes_z // 2
    into = [
        left_table(np.concatenate([cas_z[:half, c::2].T, turned_z[:half, c::2].T], 0))
        for c in range(2)
    ]
    back = [left_table(cas_z[:half, c::2]) for c in range(2)]
    ksq = signed_z[:, None] ** 2 + signed_x[None, :] ** 2
    inverse = np.where(ksq > 0, 1.0 / np.where(ksq > 0, ksq, 1.0), 0.0).astype(np.float32)
    damping = (1.0 / (1.0 + time_step * viscosity * ksq)).astype(np.float32)
    return (
        np.stack(into), np.stack(back), right_table(cas_x), right_table(slope_x), inverse, damping
    )


def kernel(
    segs, pens,
    state_hbm, krylov_hbm, into_hbm, back_hbm, cas_hbm, slope_hbm, inverse_hbm, damping_hbm,
    residual_ref, next_ref, hess_ref,
    stored, start, into_t, back_t, cas_t, slope_t, inverse, damping,
    field, wide, tall, bases, tangent, mine, theirs, ending, arrived, image,
    accum, pay, gather_pen, gather_seg, spread, pay_n, norm_pen, norm_seg,
    load_sem, local_sem, in_send, in_recv, fwd_send, swap_send, swap_recv,
    out_send, out_recv, pen_send, pen_recv, seg_send, seg_recv,
):
    seg = lax.axis_index("seg")
    pen = lax.axis_index("pen")
    planes, cut, modes_x = stored.shape[1:]
    kry = stored.shape[0]
    modes_z = cut * pens
    half = modes_z // 2
    chip = pen // 2
    core = pen % 2
    sibling = chip * 2 + 1 - core
    following = lax.rem(seg + 1, segs)
    preceding = lax.rem(seg + segs - 1, segs)

    def remote(src, dst, send, recv, to_seg, to_pen):
        return pltpu.make_async_remote_copy(
            src_ref=src, dst_ref=dst, send_sem=send, recv_sem=recv,
            device_id=(to_seg, to_pen), device_id_type=MESH,
        )

    def rows(owner):
        return pl.ds(pl.multiple_of(owner * cut, cut), cut)

    loads = [
        pltpu.make_async_copy(src, dst, load_sem.at[i])
        for i, (src, dst) in enumerate([
            (inverse_hbm, inverse), (into_hbm.at[core], into_t), (cas_hbm, cas_t),
            (slope_hbm, slope_t), (back_hbm.at[core], back_t), (damping_hbm, damping),
            (state_hbm, start), (krylov_hbm, stored),
        ])
    ]
    for load in loads:
        load.start()

    barrier = pltpu.get_barrier_semaphore()

    def greet(to_seg, to_pen):
        pl.semaphore_signal(barrier, inc=1, device_id=(to_seg, to_pen), device_id_type=MESH)

    for i in range(1, pens):
        greet(seg, lax.rem(pen + i, pens))
    for i in range(planes):
        greet(following, core * planes + i)
        greet(preceding, i * 2 + pen // planes)
    for i in range(1, segs):
        greet(lax.rem(seg + i, segs), pen)
    pl.semaphore_wait(barrier, pens - 1 + 2 * planes + segs - 1)

    sources = [lambda plane: state_hbm.at[plane], lambda plane: krylov_hbm.at[kry - 1, plane]]
    pending = []
    own = []
    for f in range(2):
        for i in range(1, planes):
            plane = lax.rem(chip + i, planes)
            copy = remote(
                sources[f](plane), field.at[f, rows(pen)], in_send.at[f, i], in_recv.at[f, pen],
                seg, plane * 2 + core,
            )
            copy.start()
            pending.append(copy)
        copy = remote(
            sources[f](chip), field.at[f, rows(pen)], in_send.at[f, 0], in_recv.at[f, pen],
            seg, sibling,
        )
        copy.start()
        pending.append(copy)
        copy = pltpu.make_async_copy(sources[f](chip), field.at[f, rows(pen)], local_sem.at[f])
        copy.start()
        own.append(copy)

    def awaited(f, owner):
        place = field.at[f, rows(owner)]
        remote(place, place, in_send.at[f, 0], in_recv.at[f, owner], seg, sibling).wait_recv()

    forwards = [[], []]

    def relay(f):
        for i in range(1, planes):
            owner = lax.rem(chip + i, planes) * 2 + core
            awaited(f, owner)
            place = field.at[f, rows(owner)]
            copy = remote(
                place, place, fwd_send.at[f, i], in_recv.at[f, owner], seg, sibling
            )
            copy.start()
            forwards[f].append(copy)

    def complete(f):
        own[f].wait()
        for i in range(planes):
            awaited(f, lax.rem(chip + i, planes) * 2 + 1 - core)

    sign = (1 - 2 * core).astype(jnp.float32)

    number = lax.broadcasted_iota(jnp.int32, (half, 1), 0)
    slope_top = number.astype(jnp.float32)
    slope_low = jnp.where(number == 0, 0, number - half).astype(jnp.float32)

    def derive(f, out):
        for way, table in ((0, slope_t), (1, cas_t)):
            for part in range(2):
                top = field[f, 0:half, :]
                low = field[f, half:modes_z, :]
                if part == 0:
                    top = top * inverse[0:half, :]
                    low = low * inverse[half:modes_z, :]
                if way == 1:
                    top = top * slope_top
                    low = low * slope_low
                high, rest = split(top + sign * low)
                lanes = slice(part * modes_x, (part + 1) * modes_x)
                wide[0:half, lanes] = high
                wide[half:modes_z, lanes] = high
                wide[modes_z:modes_z + half, lanes] = rest
            mixed = jnp.dot(
                into_t[way * half:(way + 1) * half, :], wide[...],
                preferred_element_type=jnp.float32,
            )
            for part in range(2):
                lines = slice(part * half, (part + 1) * half)
                high, rest = split(mixed[:, part * modes_x:(part + 1) * modes_x])
                tall[lines, 0:modes_x] = high
                tall[lines, modes_x:2 * modes_x] = rest
                tall[lines, 2 * modes_x:3 * modes_x] = high
            out[way] = jnp.dot(tall[...], table[...], preferred_element_type=jnp.float32)

    def swap(f, step):
        n = step * 2 + f
        return remote(
            mine.at[n], theirs.at[n], swap_send.at[n], swap_recv.at[n], seg, sibling
        )

    def give_back(f, step, value):
        high, rest = split(value)
        lanes = slice(0, modes_x)
        wide[0:half, lanes] = high
        wide[half:modes_z, lanes] = high
        wide[modes_z:modes_z + half, lanes] = rest
        mixed = jnp.dot(back_t[...], wide[:, lanes], preferred_element_type=jnp.float32)
        high, rest = split(mixed)
        lines = slice(0, half)
        tall[lines, 0:modes_x] = high
        tall[lines, modes_x:2 * modes_x] = rest
        tall[lines, 2 * modes_x:3 * modes_x] = high
        mine[step * 2 + f] = jnp.dot(
            tall[lines, :], cas_t[...], preferred_element_type=jnp.float32
        )
        swap(f, step).start()

    def base_step(step):
        base = bases.at[step]
        derive(0, base)
        upper, lower = slice(0, half), slice(half, modes_z)
        give_back(0, step, base[0, upper] * base[1, lower] - base[1, upper] * base[0, lower])

    def tangent_step(step):
        base = bases.at[step]
        derive(1, tangent)
        upper, lower = slice(0, half), slice(half, modes_z)
        give_back(
            1, step,
            tangent[0, upper] * base[1, lower] + base[0, upper] * tangent[1, lower]
            - tangent[1, upper] * base[0, lower] - base[1, upper] * tangent[0, lower],
        )

    scale = time_step / (modes_z * modes_x)

    def update(f, step):
        n = step * 2 + f
        swap(f, step).wait()
        own_part = mine[n] * scale
        other = theirs[n] * scale
        field[f, 0:half, :] = (field[f, 0:half, :] + (own_part + other)) * damping[0:half, :]
        field[f, half:modes_z, :] = (
            field[f, half:modes_z, :] + sign * (own_part - other)
        ) * damping[half:modes_z, :]

    def finish(f):
        n = (STEPS - 1) * 2 + f
        swap(f, STEPS - 1).wait()
        part = pl.ds(pl.multiple_of(core * half, half), half)
        change = jnp.where(core == 0, mine[n] + theirs[n], theirs[n] - mine[n])
        ending[f] = (field[f, part, :] + scale * change) * damping[part, :]
        for i in range(planes):
            copy = remote(
                ending.at[f, i * cut:(i + 1) * cut], arrived.at[f, chip],
                out_send.at[f, i], out_recv.at[f, chip], following, core * planes + i,
            )
            copy.start()
            pending.append(copy)

    relay(0)
    for load in loads[:5]:
        load.wait()
    complete(0)
    base_step(0)
    loads[5].wait()
    for copy in forwards[0]:
        copy.wait_send()
    for step in range(1, STEPS):
        update(0, step - 1)
        base_step(step)
    relay(1)
    finish(0)
    complete(1)
    tangent_step(0)
    for copy in forwards[1]:
        copy.wait_send()
    for step in range(1, STEPS):
        update(1, step - 1)
        tangent_step(step)
    finish(1)
    loads[6].wait()
    loads[7].wait()

    def landed(f, plane):
        remote(
            ending.at[f, 0:cut], arrived.at[f, plane], out_send.at[f, 0], out_recv.at[f, plane],
            following, pen,
        ).wait_recv()

    for plane in range(planes):
        landed(0, plane)
        residual_ref[plane] = arrived[0, plane] - start[plane]

    def fold(values):
        summed = jnp.sum(values.reshape(cut // 8, 8, modes_x), axis=0)
        total = summed[:, 0:128]
        for lane in range(128, modes_x, 128):
            total = total + summed[:, lane:lane + 128]
        return total

    for plane in range(planes):
        landed(1, plane)
        image[plane] = arrived[1, plane] - stored[kry - 1, plane]

    accum[...] = jnp.zeros_like(accum)

    def dots(plane, _):
        values = image[plane]
        for k in range(kry):
            accum[k] += fold(stored[k, plane] * values)
        return 0

    lax.fori_loop(0, planes, dots, 0)
    pay[0] = jnp.sum(accum[...], axis=1)

    def gather(source, over_pen, over_seg, turn):
        over_pen[pen] = source[0]
        copies = []
        for i in range(1, pens):
            copy = remote(
                source.at[0], over_pen.at[pen], pen_send.at[turn, i], pen_recv.at[turn, pen],
                seg, lax.rem(pen + i, pens),
            )
            copy.start()
            copies.append(copy)
        for i in range(1, pens):
            owner = lax.rem(pen + i, pens)
            remote(
                source.at[0], over_pen.at[owner], pen_send.at[turn, i],
                pen_recv.at[turn, owner], seg, owner,
            ).wait_recv()
        source[1] = jnp.sum(over_pen[...], axis=0)
        over_seg[seg] = source[1]
        for i in range(1, segs):
            copy = remote(
                source.at[1], over_seg.at[seg], seg_send.at[turn, i], seg_recv.at[turn, seg],
                lax.rem(seg + i, segs), pen,
            )
            copy.start()
            copies.append(copy)
        for i in range(1, segs):
            owner = lax.rem(seg + i, segs)
            remote(
                source.at[1], over_seg.at[owner], seg_send.at[turn, i],
                seg_recv.at[turn, owner], owner, pen,
            ).wait_recv()
        pending.extend(copies)
        return jnp.sum(over_seg[...], axis=0)

    total = float(segs * planes * modes_z * modes_x)
    coeffs = jnp.sum(gather(pay, gather_pen, gather_seg, 0), axis=1, keepdims=True) / total
    spread[...] = jnp.broadcast_to(coeffs, spread.shape)
    hess_ref[0:kry] = spread[...]

    pay_n[0] = jnp.zeros_like(pay_n[0])

    def remains(plane, _):
        values = image[plane]
        for k in range(kry):
            values = values - spread[k:k + 1, 0:1] * stored[k, plane]
        image[plane] = values
        pay_n[0] += fold(values * values)
        return 0

    lax.fori_loop(0, planes, remains, 0)
    squared = jnp.sum(gather(pay_n, norm_pen, norm_seg, 1), keepdims=True)
    norm = jnp.sqrt(squared / total + 1e-06)
    hess_ref[kry:kry + 8] = jnp.broadcast_to(norm, (8, 128))
    factor = 1.0 / norm
    for plane in range(planes):
        next_ref[plane] = image[plane] * factor
    for copy in pending:
        copy.wait_send()


def fused(state, krylov, *, tables_of, segs, pens):
    planes, cut, modes_x = state.shape
    kry = krylov.shape[0]
    modes_z = cut * pens
    half = modes_z // 2
    f32, bf16 = jnp.float32, jnp.bfloat16
    dma = pltpu.SemaphoreType.DMA
    vmem = pltpu.VMEM
    residual, next_vector, hess = pl.pallas_call(
        functools.partial(kernel, segs, pens),
        out_shape=(
            jax.ShapeDtypeStruct(state.shape, f32),
            jax.ShapeDtypeStruct(state.shape, f32),
            jax.ShapeDtypeStruct((kry + 8, 128), f32),
        ),
        in_specs=[pl.BlockSpec(memory_space=pltpu.HBM)] * 8,
        out_specs=(pl.BlockSpec(memory_space=pltpu.VMEM),) * 3,
        scratch_shapes=[
            vmem(krylov.shape, f32),
            vmem(state.shape, f32),
            vmem((modes_z, 3 * half), bf16),
            vmem((half, 3 * half), bf16),
            vmem((3 * modes_x, modes_x), bf16),
            vmem((3 * modes_x, modes_x), bf16),
            vmem((modes_z, modes_x), f32),
            vmem((modes_z, modes_x), f32),
            vmem((2, modes_z, modes_x), f32),
            vmem((3 * half, 2 * modes_x), bf16),
            vmem((modes_z, 3 * modes_x), bf16),
            vmem((STEPS, 2, modes_z, modes_x), f32),
            vmem((2, modes_z, modes_x), f32),
            vmem((2 * STEPS, half, modes_x), f32),
            vmem((2 * STEPS, half, modes_x), f32),
            vmem((2, half, modes_x), f32),
            vmem((2, planes, cut, modes_x), f32),
            vmem((planes, cut, modes_x), f32),
            vmem((kry, 8, 128), f32),
            vmem((2, kry, 128), f32),
            vmem((pens, kry, 128), f32),
            vmem((segs, kry, 128), f32),
            vmem((kry, 128), f32),
            vmem((2, 8, 128), f32),
            vmem((pens, 8, 128), f32),
            vmem((segs, 8, 128), f32),
            dma((8,)),
            dma((2,)),
            dma((2, planes)),
            dma((2, pens)),
            dma((2, planes)),
            dma((2 * STEPS,)),
            dma((2 * STEPS,)),
            dma((2, planes)),
            dma((2, planes)),
            dma((2, pens)),
            dma((2, pens)),
            dma((2, segs)),
            dma((2, segs)),
        ],
        compiler_params=pltpu.CompilerParams(
            collective_id=0, has_side_effects=True, vmem_limit_bytes=63_400_000
        ),
    )(state, krylov, *[jnp.asarray(t) for t in tables_of])
    return residual, next_vector, hess[:kry + 1, 0]


def solution(mesh):
    segs, pens = mesh.shape["seg"], mesh.shape["pen"]

    def whole(state, krylov):
        rows, modes_z, modes_x = state.shape
        planes, cut = rows // segs, modes_z // pens
        local = body
        if (
            pens == 2 * planes
            and cut % 8 == 0
            and modes_z % 32 == 0
            and modes_x % 128 == 0
            and krylov.shape[0] % 8 == 0
        ):
            local = functools.partial(
                fused, tables_of=constants(modes_z, modes_x), segs=segs, pens=pens
            )
        return jax.shard_map(
            local,
            mesh=mesh,
            in_specs=(P("seg", "pen", None), P(None, "seg", "pen", None)),
            out_specs=(P("seg", "pen", None), P("seg", "pen", None), P()),
            check_vma=False,
        )(state, krylov)

    return whole
```
